512 devices in a mesh: gx: 64 (over x, z_lo, core), gy: 8 (over y, z_hi).
Axes of the slice: x: 4, y: 4, z: 16 (z_hi: 2, z_lo: 8; z = z_hi * 8 + z_lo), core: 2. Of those that a mesh axis runs over, the one named last changes fastest.
Arguments:
- normals: float32 [1, 2, 4096, 4096], P(None, None, 'gx', 'gy'), may hold values from -6 to 6
- plane_length: float32 [2], replicated, may hold values from 2 to 32
- plane_amplitude: float32 [2], replicated, may hold values from 0.4 to 1.4
- plane_mean: float32 [2], replicated, may hold values from -1 to 1
Outputs:
- coarse_log: float32 [1, 1, 2048, 2048], P(None, None, 'gx', 'gy')
The draws below stay inside these ranges and needn't reach their ends.
All inputs are finite; a program needn't handle non-finite values.
Results may differ from the reference program's by a relative error of at most 0.000088.
Values sent between devices are 32-bit elements; how exact they have to be, the bound alone decides.
No kernel may reach another device: no remote copies, remote signals or barrier semaphores. Data moves between devices by JAX's collectives and lax.ppermute only.
A program may use at most 64 MiB of HBM per device.

```python
import math
import jax
import jax.numpy as jnp
from jax import lax

NX = 4096
NY = 4096
REALS = 1
PLANES = 2


def level_of(rng, shape, split, least, top_value):
    level, own = 1.0, jax.random.fold_in(rng, 6)
    for dim, blocks in split:
        draws = jnp.exp(jax.random.uniform(jax.random.fold_in(own, dim), (blocks,), jnp.float32, least / len(split), top_value / len(split)))
        level = level * jnp.repeat(draws, shape[dim] // blocks).reshape([-1 if axis == dim else 1 for axis in range(len(shape))])
    return level


def normal_values(rng, extent, deviation, reach, split=(), kind=jnp.bfloat16):
    values = deviation * jax.random.normal(rng, extent, jnp.float32)
    if split:
        values = values * level_of(rng, extent, split, -0.22, 0.18)
    return jnp.clip(values, -reach, reach).astype(kind)


def setup_inputs(seed: int = 0) -> dict:
    streams_of = jax.random.split(jax.random.key(seed), 5)
    return {
        "normals": normal_values(streams_of[0], (REALS, PLANES, NX, NY), 1.0, 6.0, ((2, 64), (3, 8)), jnp.float32),
        "plane_length": jnp.clip(jnp.exp(jax.random.uniform(streams_of[1], (PLANES,), jnp.float32, math.log(2.0), math.log(32.0))), 2.0, 32.0),
        "plane_amplitude": jnp.clip(jnp.exp(jax.random.uniform(streams_of[2], (PLANES,), jnp.float32, math.log(0.4), math.log(1.4))), 0.4, 1.4),
        "plane_mean": jnp.clip(jax.random.uniform(streams_of[3], (PLANES,), jnp.float32, -1.0, 1.0), -1.0, 1.0),
    }


def inverse_cosine(values):
    length = values.shape[-1]
    wave_index = jnp.arange(length, dtype=jnp.float32)
    weight = jnp.where(wave_index == 0, jnp.sqrt(1.0 / length), jnp.sqrt(2.0 / length)).astype(jnp.float32)
    phases = wave_index * (math.pi / (2 * length))
    weighted = values * weight
    complex_terms = weighted * jnp.cos(phases) + 1j * (weighted * jnp.sin(phases))
    padded = jnp.concatenate([complex_terms, jnp.zeros_like(complex_terms)], axis=-1)
    return jnp.real(jnp.fft.ifft(padded, axis=-1))[..., :length] * (2 * length)

def reference(normals, plane_length, plane_amplitude, plane_mean):
    wave_x = jnp.arange(NX, dtype=jnp.float32) / NX
    wave_y = jnp.arange(NY, dtype=jnp.float32) / NY
    radius = wave_x[:, None] ** 2 + wave_y[None, :] ** 2
    pairs = REALS * PLANES // 2
    norming = math.sqrt(2.0 * math.pi) / math.sqrt(NX * NY)
    flat_normals = normals.reshape(pairs, 2, NX, NY)
    lengths = jnp.tile(plane_length.reshape(PLANES // 2, 2), (REALS, 1))
    amplitudes = jnp.tile(plane_amplitude.reshape(PLANES // 2, 2), (REALS, 1))
    means = jnp.tile(plane_mean.reshape(PLANES // 2, 2), (REALS, 1))

    def one_pair(inputs):
        values, pair_length, pair_amplitude, pair_mean = inputs
        denominator = 1.0 + ((math.pi * pair_length) ** 2)[:, None, None] * radius[None]
        factor = pair_amplitude * pair_length * norming
        spectrum = factor[:, None, None] * jnp.power(denominator, -0.75)
        scaled = spectrum * values
        along_second = inverse_cosine(scaled)
        field = jnp.swapaxes(inverse_cosine(jnp.swapaxes(along_second, 1, 2)), 1, 2)
        log_perm = field + pair_mean[:, None, None]
        blocks = jnp.exp(-log_perm).reshape(2, NX // 2, 2, NY // 2, 2)
        return -jnp.log(lax.optimization_barrier(jnp.mean(blocks, axis=(0, 2, 4))))
    coarse = lax.map(one_pair, (flat_normals, lengths, amplitudes, means))
    return coarse.reshape(REALS, PLANES // 2, NX // 2, NY // 2)
```

```python
import math

import jax
import jax.numpy as jnp
import numpy as np
from jax import lax
from jax.experimental import pallas as pl
from jax.experimental.pallas import tpu as pltpu
from jax.sharding import PartitionSpec as P

F32 = jnp.float32
BF16 = jnp.bfloat16
NX = 4096
NY = 4096
GX = 64
GY = 8
NN = (((1,), (0,)), ((), ()))
NT = (((1,), (1,)), ((), ()))
TN = (((0,), (0,)), ((), ()))


def np_split(table):
    high = table.astype(np.float32).astype(jnp.bfloat16)
    low = (table - high.astype(np.float64)).astype(np.float32).astype(jnp.bfloat16)
    return high, low


def split(values):
    high = values.astype(BF16)
    low = (values - high.astype(F32)).astype(BF16)
    return high, low


def mul(left, right, dims):
    return lax.dot_general(left, right, dims, preferred_element_type=F32)


def angles(top, period):
    return np.pi * (top % (2 * period)).astype(np.float64) / period


def y_tables():
    outer, inner = 32, 128
    a = np.arange(outer)[None, :]
    l = np.arange(outer)[:, None]
    first = angles(a * (2 * l + 1), 2 * outer)
    first = np.concatenate([np.cos(first), np.sin(first)], 0)
    high, low = np_split(first)
    first = np.concatenate([high, high, low], 1)
    b = np.arange(inner)[None, :]
    turn = angles(b * (2 * l + 1), 2 * NY)
    turn = np.stack([np.cos(turn), np.sin(turn)]).astype(np.float32)
    sub, j = np.meshgrid(np.arange(16), np.arange(GY), indexing="ij")
    m = np.where(sub < 8, 8 * j + sub, 127 - 8 * j - (sub - 8)).reshape(-1, 1)
    last = angles(2 * b * m, inner)
    last = np.concatenate([np.cos(last), -np.sin(last)], 1)
    return first, turn, np.concatenate(np_split(last), 0)


def x_tables():
    outer, inner = 512, 8
    l = np.concatenate([np.arange(0, 256, 2), np.arange(1, 256, 2)])[:, None]
    parts = []
    for odd in range(2):
        a = 2 * np.arange(256)[None, :] + odd
        phase = angles(a * (2 * l + 1), 2 * outer)
        parts.append(np.concatenate(np_split(np.concatenate([np.cos(phase), np.sin(phase)], 0)), 0))
    first = np.stack(parts)
    l = l[:, 0]
    rows = np.concatenate([l[:128], 511 - l[128:], l[128:], 511 - l[:128]])[:, None]
    lanes = np.arange(128)[None, :]
    b = lanes // 8 % 8
    turn = angles(b * (2 * rows + 1), 2 * NX)
    turn = np.stack([np.cos(turn), np.sin(turn)]).astype(np.float32)
    index = np.arange(128)[:, None]
    plane, fine = index // 64, index // 8 % 4 * 2 + index // 32 % 2
    m = np.array([0, 1, 2, 3, 7, 6, 5, 4])[index % 8]
    same = 1.0 * ((lanes // 64 == plane) & (lanes % 8 == fine))
    phase = angles(2 * b * m, inner)
    last = np.concatenate([same * np.cos(phase), -same * np.sin(phase)], 1)
    return first, turn, np.concatenate(np_split(last), 0)


def place_table():
    src = np.arange(GX)
    octet, sub = src // 16, src % 16
    table = np.zeros((GX, 4, 256), np.float32)
    for ly in range(4):
        column = np.where(sub < 8, 32 * sub + 4 * octet + ly, 32 * (sub - 8) + 31 - 4 * octet - ly)
        table[src, ly, column] = 1
    return np.concatenate([table.reshape(GX, 1024)] * 3, 0).astype(jnp.bfloat16)


def scale_kernel(ids, length, amplitude, x_ref, o_ref):
    norming = math.sqrt(2.0 * math.pi) / math.sqrt(NX * NY)
    row = ids[0] * 64 + lax.broadcasted_iota(jnp.int32, (64, 128), 0)
    row_wave = row.astype(F32) * (1.0 / NX)
    row_weight = jnp.where(row == 0, math.sqrt(1.0 / NX), math.sqrt(2.0 / NX))
    for c in range(4):
        col = ids[1] * 512 + c * 128 + lax.broadcasted_iota(jnp.int32, (64, 128), 1)
        col_wave = col.astype(F32) * (1.0 / NY)
        weight = row_weight * jnp.where(col == 0, math.sqrt(1.0 / NY), math.sqrt(2.0 / NY))
        radius = row_wave * row_wave + col_wave * col_wave
        for p in range(2):
            reach = math.pi * length[p]
            root = lax.rsqrt(1.0 + reach * reach * radius)
            factor = amplitude[p] * length[p] * norming
            spectrum = factor * (root * jnp.sqrt(root))
            scaled = x_ref[0, p, :, c * 128:(c + 1) * 128] * spectrum * weight
            o_ref[:, c, p] = scaled.reshape(8, 8, 128)


def y_kernel(x_ref, first_ref, turn_ref, last_ref, o_ref, w_ref):
    pieces = []
    for line in range(16):
        high, low = split(x_ref[pl.ds(line, 32, stride=16), :])
        pieces.append(jnp.concatenate([high, low, high], 0))
    part = mul(first_ref[...], jnp.concatenate(pieces, 1), NN)
    turn_c, turn_s = turn_ref[0], turn_ref[1]
    for line in range(16):
        block = part[:, line * 128:(line + 1) * 128]
        part_c, part_s = block[:32], block[32:]
        w_ref[:, line, :, :128] = (part_c * turn_c - part_s * turn_s).reshape(4, 8, 128)
        w_ref[:, line, :, 128:] = (part_c * turn_s + part_s * turn_c).reshape(4, 8, 128)
    high, low = split(w_ref[...].reshape(512, 256))
    both = mul(last_ref[...], high, NT)
    out = both[:128] + both[128:] + mul(last_ref[:128, :], low, NT)
    for octet in range(4):
        o_ref[octet * 128:(octet + 1) * 128, :] = out[:, octet * 128:(octet + 1) * 128]


def x_kernel(mean, x_ref, first_ref, turn_ref, last_ref, o_ref):
    halves = []
    for odd in range(2):
        values = x_ref[pl.ds(odd, 256, stride=2), :]
        both = mul(first_ref[odd], jnp.concatenate(split(values), 1), NN)
        halves.append(both[:512, :128] + (both[:512, 128:] + both[512:, :128]))
    (even_c, even_s), (odd_c, odd_s) = [(h[:256], h[256:]) for h in halves]
    plus_c, minus_c = even_c + odd_c, even_c - odd_c
    plus_s, minus_s = even_s + odd_s, odd_s - even_s
    part_c = jnp.concatenate([plus_c[:128], minus_c[128:], plus_c[128:], minus_c[:128]], 0)
    part_s = jnp.concatenate([plus_s[:128], minus_s[128:], plus_s[128:], minus_s[:128]], 0)
    turn_c, turn_s = turn_ref[0], turn_ref[1]
    turned = jnp.concatenate(
        [part_c * turn_c - part_s * turn_s, part_c * turn_s + part_s * turn_c], 1
    )
    high, low = split(turned)
    both = mul(last_ref[...], high, NT)
    field = both[:128] + both[128:] + mul(last_ref[:128, :], low, NT)
    total = jnp.zeros((32, 512), F32)
    for p in range(2):
        values = jnp.exp(-(field[64 * p:64 * p + 64] + mean[p]))
        total = total + values[:32] + values[32:]
    coarse = -jnp.log((total[:, :256] + total[:, 256:]) * 0.125)
    group = lax.broadcasted_iota(jnp.int32, (8, 128), 1) // 32
    for half in range(2):
        blocks = [coarse[8 * ly:8 * ly + 8, 128 * half:128 * half + 128] for ly in range(4)]
        for q in range(4):
            row = blocks[q]
            for ly in range(4):
                if ly != q:
                    row = jnp.where(group == ly, pltpu.roll(blocks[ly], (ly - q) * 32 % 128, 1), row)
            block = 7 - q if half else q
            o_ref[:, block, :] = row[:4]
            o_ref[:, 15 - block, :] = row[4:]


def place_kernel(ids, x_ref, table_ref, o_ref):
    values = x_ref[...]
    high, rest = values.astype(BF16), values - values.astype(BF16).astype(F32)
    middle, low = split(rest)
    spread = mul(jnp.concatenate([high, middle, low], 0), table_ref[...], TN)
    out = spread[:32, :256]
    for ly in range(1, 4):
        out = out + spread[32 * ly:32 * ly + 32, 256 * ly:256 * ly + 256]
    back = ids[0] // 4 % 2
    for r in range(32):
        o_ref[pl.ds(jnp.where(back == 1, 31 - r, r), 1), :] = out[r:r + 1]


def call(kernel, shape, places, scratch=(), cost=None):
    spaces = {"s": pltpu.SMEM, "v": pltpu.VMEM}
    return pl.pallas_call(
        kernel,
        out_shape=jax.ShapeDtypeStruct(shape, F32),
        in_specs=[pl.BlockSpec(memory_space=spaces[place]) for place in places],
        out_specs=pl.BlockSpec(memory_space=pltpu.VMEM),
        scratch_shapes=list(scratch),
        compiler_params=pltpu.CompilerParams(vmem_limit_bytes=32 * 1024 * 1024),
    )


def body(normals, plane_length, plane_amplitude, plane_mean):
    ids = jnp.stack([lax.axis_index("gx"), lax.axis_index("gy")]).astype(jnp.int32)
    scaled = call(scale_kernel, (8, 4, 2, 8, 128), "sssv")(
        ids, plane_length, plane_amplitude, normals
    )
    lines = lax.all_to_all(scaled.reshape(8, 64, 128), "gy", 0, 0, tiled=True)
    first, turn, last = y_tables()
    rows = call(y_kernel, (512, 128), "vvvv", [pltpu.VMEM((4, 16, 8, 256), F32)])(
        lines.reshape(512, 128), first, turn, last
    )
    rows = lax.all_to_all(rows.reshape(512, 1, 128), ("gx", "gy"), 0, 0, tiled=True)
    first, turn, last = x_tables()
    coarse = call(x_kernel, (4, 16, 128), "svvvv")(
        plane_mean, rows.reshape(512, 128), first, turn, last
    )
    coarse = lax.all_to_all(coarse.reshape(64, 1, 128), "gx", 0, 0, tiled=True)
    out = call(place_kernel, (32, 256), "svv")(ids, coarse.reshape(64, 128), place_table())
    return out.reshape(1, 1, 32, 256)


def solution(mesh):
    return jax.shard_map(
        body,
        mesh=mesh,
        in_specs=(P(None, None, "gx", "gy"), P(), P(), P()),
        out_specs=P(None, None, "gx", "gy"),
        check_vma=False,
    )
```

```python
import math

import jax
import jax.numpy as jnp
import numpy as np
from jax import lax
from jax.experimental import pallas as pl
from jax.experimental.pallas import tpu as pltpu
from jax.sharding import PartitionSpec as P

F32 = jnp.float32
BF16 = jnp.bfloat16
NX = 4096
NY = 4096
GX = 64
GY = 8
NN = (((1,), (0,)), ((), ()))
NT = (((1,), (1,)), ((), ()))
TN = (((0,), (0,)), ((), ()))


def np_split(table):
    high = table.astype(np.float32).astype(jnp.bfloat16)
    low = (table - high.astype(np.float64)).astype(np.float32).astype(jnp.bfloat16)
    return high, low


def split(values):
    high = values.astype(BF16)
    low = (values - high.astype(F32)).astype(BF16)
    return high, low


def mul(left, right, dims):
    return lax.dot_general(left, right, dims, preferred_element_type=F32)


def angles(top, period):
    return np.pi * (top % (2 * period)).astype(np.float64) / period


def y_tables():
    outer, inner = 32, 128
    a = np.arange(outer).reshape(4, 2, 4).transpose(1, 0, 2).reshape(1, outer)
    l = np.arange(outer)[:, None]
    phase = angles(a * (2 * l + 1), 2 * outer)
    high, low = [t.astype(np.float64) for t in np_split(np.concatenate([np.cos(phase), np.sin(phase)], 0))]
    b = np.arange(inner)[None, :]
    turn = angles(b * (2 * l + 1), 2 * NY)
    turn = np.concatenate([np.cos(turn), np.sin(turn)], 1)
    sub, j = np.meshgrid(np.arange(16), np.arange(GY), indexing="ij")
    m = np.where(sub < 8, 8 * j + sub, 127 - 8 * j - (sub - 8)).reshape(-1, 1)
    last = angles(2 * b * m, inner)
    last = np.concatenate([np.cos(last), -np.sin(last)], 1)
    packed = np.zeros((288, 256))
    for h in range(2):
        own = slice(16 * h, 16 * h + 16)
        packed[64 * h:64 * h + 64, :48] = np.concatenate([high[:, own], high[:, own], low[:, own]], 1)
    packed[128:160] = turn
    packed[160:] = last
    return packed.astype(np.float32)


def x_tables():
    outer, inner = 256, 16
    l = np.concatenate([np.arange(0, outer, 2), np.arange(1, outer, 2)])[:, None]
    phase = angles(np.arange(outer)[None, :] * (2 * l + 1), 2 * outer)
    first = np.concatenate(np_split(np.concatenate([np.cos(phase), np.sin(phase)], 0)), 0)
    lanes = np.arange(128)[None, :]
    b = lanes // 8
    turn = angles(b * (2 * l + 1), 2 * NX)
    turn = np.stack([np.cos(turn), np.sin(turn)]).astype(np.float32)
    index = np.arange(128)[:, None]
    fine = index // 16 % 4 * 2 + index // 64
    m = np.concatenate([np.arange(8), np.arange(15, 7, -1)])[index % 16]
    same = 1.0 * (lanes % 8 == fine)
    phase = angles(2 * b * m, inner)
    last = np.concatenate([same * np.cos(phase), -same * np.sin(phase)], 1)
    return first, turn, np.concatenate(np_split(last), 0)


def place_table():
    src = np.arange(GX)
    octet, sub = src // 16, src % 16
    table = np.zeros((GX, 4, 256), np.float32)
    for ly in range(4):
        column = np.where(sub < 8, 32 * sub + 4 * octet + ly, 32 * (sub - 8) + 31 - 4 * octet - ly)
        table[src, ly, column] = 1
    return np.concatenate([table.reshape(GX, 1024)] * 3, 0).astype(jnp.bfloat16)


def scale_kernel(ids, length_in, amplitude_in, mean_in, x_in, o_ref, mean_ref, length, amplitude, mean, x_ref, sems):
    moves = [
        pltpu.make_async_copy(source, target, sems.at[k])
        for k, (source, target) in enumerate(
            [(x_in, x_ref), (length_in, length), (amplitude_in, amplitude), (mean_in, mean)]
        )
    ]
    for move in moves:
        move.start()
    norming = math.sqrt(2.0 * math.pi) / math.sqrt(NX * NY)
    row = ids[0] * 64 + lax.broadcasted_iota(jnp.int32, (64, 128), 0)
    row_wave = row.astype(F32) * (1.0 / NX)
    row_wave = row_wave * row_wave
    row_weight = jnp.where(row == 0, math.sqrt(1.0 / NX), math.sqrt(2.0 / NX))
    for move in moves:
        move.wait()
    for c in range(4):
        col = ids[1] * 512 + c * 128 + lax.broadcasted_iota(jnp.int32, (64, 128), 1)
        col_wave = col.astype(F32) * (1.0 / NY)
        weight = row_weight * jnp.where(col == 0, math.sqrt(1.0 / NY), math.sqrt(2.0 / NY))
        radius = row_wave + col_wave * col_wave
        for p in range(2):
            reach = math.pi * length[p]
            root = lax.rsqrt(1.0 + reach * reach * radius)
            factor = amplitude[p] * length[p] * norming
            spectrum = factor * (root * jnp.sqrt(root))
            scaled = x_ref[0, p, :, c * 128:(c + 1) * 128] * spectrum * weight
            o_ref[:, c, p] = scaled.reshape(4, 16, 128)
    for p in range(2):
        mean_ref[p] = jnp.full((8, 128), mean[p], F32)


def y_kernel(ids, x_ref, table_ref, o_ref, w_ref):
    half = ids[1] % 2
    first = table_ref[pl.ds(pl.multiple_of(half * 64, 64), 64), :128].astype(BF16)[:, :48]
    turn_c, turn_s = table_ref[128:160, :128], table_ref[128:160, 128:]
    last = jnp.concatenate(split(table_ref[160:288, :]), 0)
    for group in range(4):
        pieces = []
        for line in range(8 * group, 8 * group + 8):
            high, low = split(x_ref[pl.ds(line, 16, stride=32), :])
            pieces.append(jnp.concatenate([high, low, high], 0))
        part = mul(first, jnp.concatenate(pieces, 1), NN)
        for k in range(8):
            part_c, part_s = part[:32, k * 128:(k + 1) * 128], part[32:, k * 128:(k + 1) * 128]
            line = 8 * group + k
            w_ref[:, line, :, :128] = (part_c * turn_c - part_s * turn_s).reshape(4, 8, 128)
            w_ref[:, line, :, 128:] = (part_c * turn_s + part_s * turn_c).reshape(4, 8, 128)
    for octet in range(4):
        high, low = split(w_ref[octet].reshape(256, 256))
        both = mul(last, high, NT)
        out = both[:128] + both[128:] + mul(last[:128], low, NT)
        for p in range(2):
            o_ref[pl.ds(octet * 256 + p, 128, stride=2), :] = out[:, p * 128:(p + 1) * 128]


def x_kernel(mean_ref, x_ref, first_ref, turn_ref, last_ref, o_ref):
    total = jnp.zeros((64, 128), F32)
    turn_c, turn_s = turn_ref[0], turn_ref[1]
    for p in range(2):
        values = x_ref[pl.ds(p, 256, stride=4), :] + x_ref[pl.ds(p + 2, 256, stride=4), :]
        both = mul(first_ref[...], jnp.concatenate(split(values), 1), NN)
        part = both[:512, :128] + (both[:512, 128:] + both[512:, :128])
        part_c, part_s = part[:256], part[256:]
        turned = jnp.concatenate(
            [part_c * turn_c - part_s * turn_s, part_c * turn_s + part_s * turn_c], 1
        )
        high, low = split(turned)
        both = mul(last_ref[...], high, NT)
        field = both[:128] + both[128:] + mul(last_ref[:128, :], low, NT)
        for side in range(2):
            values = jnp.exp(-(field[:, 128 * side:128 * side + 128] + mean_ref[p, 0:1, :]))
            total = total + values[:64] + values[64:]
    coarse = -jnp.log(total * 0.125)
    group = lax.broadcasted_iota(jnp.int32, (16, 128), 1) // 32
    blocks = [coarse[16 * ly:16 * ly + 16] for ly in range(4)]
    for q in range(4):
        row = blocks[q]
        for ly in range(4):
            if ly != q:
                row = jnp.where(group == ly, pltpu.roll(blocks[ly], (ly - q) * 32 % 128, 1), row)
        o_ref[:, q, :] = row[:8]
        o_ref[:, 7 - q, :] = row[8:]


def place_kernel(ids, x_ref, table_ref, o_ref):
    values = x_ref[...]
    high, rest = values.astype(BF16), values - values.astype(BF16).astype(F32)
    middle, low = split(rest)
    spread = mul(jnp.concatenate([high, middle, low], 0), table_ref[...], TN)
    out = spread[:32, :256]
    for ly in range(1, 4):
        out = out + spread[32 * ly:32 * ly + 32, 256 * ly:256 * ly + 256]
    back = ids[0] // 4 % 2
    for r in range(32):
        o_ref[pl.ds(jnp.where(back == 1, 31 - r, r), 1), :] = out[r:r + 1]


def call(kernel, shapes, places, scratch=()):
    spaces = {"s": pltpu.SMEM, "v": pltpu.VMEM, "h": pltpu.HBM}
    outs = [jax.ShapeDtypeStruct(shape, F32) for shape in shapes]
    result = pl.pallas_call(
        kernel,
        out_shape=outs,
        in_specs=[pl.BlockSpec(memory_space=spaces[place]) for place in places],
        out_specs=[pl.BlockSpec(memory_space=pltpu.VMEM)] * len(outs),
        scratch_shapes=list(scratch),
        compiler_params=pltpu.CompilerParams(vmem_limit_bytes=32 * 1024 * 1024),
    )
    return lambda *operands: result(*operands)


def body(normals, plane_length, plane_amplitude, plane_mean):
    ids = jnp.stack([lax.axis_index("gx"), lax.axis_index("gy")]).astype(jnp.int32)
    scratch = [pltpu.SMEM((2,), F32)] * 3 + [pltpu.VMEM((1, 2, 64, 512), F32), pltpu.SemaphoreType.DMA((4,))]
    scaled, mean = call(scale_kernel, [(4, 4, 2, 16, 128), (2, 8, 128)], "shhhh", scratch)(
        ids, plane_length, plane_amplitude, plane_mean, normals
    )
    sides = [[2 * y + h for y in range(4)] for h in range(2)]
    lines = lax.all_to_all(
        scaled.reshape(4, 128, 128), "gy", 0, 0, tiled=True, axis_index_groups=sides
    )
    (rows,) = call(y_kernel, [(1024, 128)], "svv", [pltpu.VMEM((4, 32, 8, 256), F32)])(
        ids, lines.reshape(512, 128), y_tables()
    )
    rows = lax.all_to_all(rows.reshape(512, 2, 128), ("gx", "gy"), 0, 0, tiled=True)
    first, turn, last = x_tables()
    (coarse,) = call(x_kernel, [(8, 8, 128)], "vvvvv")(
        mean, rows.reshape(1024, 128), first, turn, last
    )
    coarse = lax.all_to_all(coarse.reshape(64, 1, 128), "gx", 0, 0, tiled=True)
    (out,) = call(place_kernel, [(32, 256)], "svv")(ids, coarse.reshape(64, 128), place_table())
    return out.reshape(1, 1, 32, 256)


def solution(mesh):
    return jax.shard_map(
        body,
        mesh=mesh,
        in_specs=(P(None, None, "gx", "gy"), P(), P(), P()),
        out_specs=P(None, None, "gx", "gy"),
        check_vma=False,
    )
```

```python
import math

import jax
import jax.numpy as jnp
import numpy as np
from jax import lax
from jax.experimental import pallas as pl
from jax.experimental.pallas import tpu as pltpu
from jax.sharding import PartitionSpec as P

F32 = jnp.float32
BF16 = jnp.bfloat16
NX = 4096
NY = 4096
GX = 64
GY = 8
NN = (((1,), (0,)), ((), ()))
NT = (((1,), (1,)), ((), ()))


def np_split(table):
    high = table.astype(np.float32).astype(jnp.bfloat16)
    low = (table - high.astype(np.float64)).astype(np.float32).astype(jnp.bfloat16)
    return high, low


def split(values):
    high = values.astype(BF16)
    low = (values - high.astype(F32)).astype(BF16)
    return high, low


def mul(left, right, dims):
    return lax.dot_general(left, right, dims, preferred_element_type=F32)


def angles(top, period):
    return np.pi * (top % (2 * period)).astype(np.float64) / period


def y_tables():
    outer, inner = 32, 128
    a = np.arange(outer).reshape(4, 2, 4).transpose(1, 0, 2).reshape(1, outer)
    l = np.arange(outer)[:, None]
    phase = angles(a * (2 * l + 1), 2 * outer)
    high, low = [t.astype(np.float64) for t in np_split(np.concatenate([np.cos(phase), np.sin(phase)], 0))]
    b = np.arange(inner)[None, :]
    turn = angles(b * (2 * l + 1), 2 * NY)
    turn = np.concatenate([np.cos(turn), np.sin(turn)], 1)
    j, sub = np.meshgrid(np.arange(GY), np.arange(16), indexing="ij")
    m = np.where(sub < 8, 8 * j + sub, 127 - 8 * j - (sub - 8)).reshape(-1, 1)
    last = angles(2 * b * m, inner)
    last = np.concatenate([np.cos(last), -np.sin(last)], 1)
    packed = np.zeros((288, 256))
    for h in range(2):
        own = slice(16 * h, 16 * h + 16)
        packed[64 * h:64 * h + 64, :48] = np.concatenate([high[:, own], high[:, own], low[:, own]], 1)
    packed[128:160] = turn
    packed[160:] = last
    return packed.astype(np.float32)


def x_tables():
    outer, inner = 256, 16
    l = np.concatenate([np.arange(0, outer, 2), np.arange(1, outer, 2)])[:, None]
    a = np.arange(outer).reshape(64, 2, 2).transpose(1, 0, 2).reshape(1, outer)
    phase = angles(a * (2 * l + 1), 2 * outer)
    first = np.concatenate(np_split(np.concatenate([np.cos(phase), np.sin(phase)], 0)), 0)
    lanes = np.arange(128)[None, :]
    b = lanes // 8
    turn = angles(b * (2 * l + 1), 2 * NX)
    turn = np.stack([np.cos(turn), np.sin(turn)]).astype(np.float32)
    index = np.arange(128)[:, None]
    fine = index // 16 % 4 * 2 + index // 64
    m = np.concatenate([np.arange(8), np.arange(15, 7, -1)])[index % 16]
    same = 1.0 * (lanes % 8 == fine)
    phase = angles(2 * b * m, inner)
    last = np.concatenate([same * np.cos(phase), -same * np.sin(phase)], 1)
    return first, turn, np.concatenate(np_split(last), 0)


def place_table():
    src = np.arange(GX)
    octet, sub = src // 16, src % 16
    table = np.zeros((GX, 4, 256), np.float32)
    for ly in range(4):
        column = np.where(sub < 8, 32 * sub + 4 * octet + ly, 32 * (sub - 8) + 31 - 4 * octet - ly)
        table[src, ly, column] = 1
    return table.reshape(GX, 1024).astype(jnp.bfloat16)


def y_kernel(length, amplitude, mean, x_ref, table_ref, o_ref, mean_ref, s_ref, w_ref):
    gx, gy = lax.axis_index("gx"), lax.axis_index("gy")
    plane, half = gy // 4, gy % 2
    norming = math.sqrt(2.0 * math.pi) / math.sqrt(NX * NY)
    row = gx * 64 + gy // 2 % 2 * 32 + lax.broadcasted_iota(jnp.int32, (32, 128), 0)
    row_wave = row.astype(F32) * (1.0 / NX)
    row_wave = row_wave * row_wave
    row_weight = jnp.where(row == 0, math.sqrt(1.0 / NX), math.sqrt(2.0 / NX))
    lane = lax.broadcasted_iota(jnp.int32, (32, 128), 1)
    reach = math.pi * length[plane]
    factor = amplitude[plane] * length[plane] * norming
    for a in range(16):
        col = (a // 4 * 8 + half * 4 + a % 4) * 128 + lane
        col_wave = col.astype(F32) * (1.0 / NY)
        weight = row_weight * jnp.where(col == 0, math.sqrt(1.0 / NY), math.sqrt(2.0 / NY))
        root = lax.rsqrt(1.0 + reach * reach * (row_wave + col_wave * col_wave))
        spectrum = factor * (root * jnp.sqrt(root))
        block = x_ref[a // 4, :, a % 4 * 128:a % 4 * 128 + 128]
        s_ref[32 * a:32 * a + 32, :] = block * spectrum * weight
    for p in range(2):
        mean_ref[p] = jnp.full((8, 128), mean[p], F32)
    first = table_ref[pl.ds(pl.multiple_of(half * 64, 64), 64), :128].astype(BF16)[:, :48]
    turn_c, turn_s = table_ref[128:160, :128], table_ref[128:160, 128:]
    last = jnp.concatenate(split(table_ref[160:288, :]), 0)
    for group in range(4):
        pieces = []
        for line in range(8 * group, 8 * group + 8):
            high, low = split(s_ref[pl.ds(line, 16, stride=32), :])
            pieces.append(jnp.concatenate([high, low, high], 0))
        part = mul(first, jnp.concatenate(pieces, 1), NN)
        for k in range(8):
            part_c, part_s = part[:32, k * 128:(k + 1) * 128], part[32:, k * 128:(k + 1) * 128]
            line = 8 * group + k
            w_ref[:, line, :, :128] = (part_c * turn_c - part_s * turn_s).reshape(4, 8, 128)
            w_ref[:, line, :, 128:] = (part_c * turn_s + part_s * turn_c).reshape(4, 8, 128)
    for octet in range(4):
        high, low = split(w_ref[octet].reshape(256, 256))
        both = mul(last, high, NT)
        out = both[:128] + both[128:] + mul(last[:128], low, NT)
        for j in range(GY):
            for side in range(2):
                block = out[16 * j:16 * j + 16, 128 * side:128 * side + 128]
                o_ref[pl.ds(128 * j + 32 * octet + side, 16, stride=2), :] = block


def x_kernel(mean_ref, x_ref, first_ref, turn_ref, last_ref, o_ref):
    total = jnp.zeros((64, 128), F32)
    turn_c, turn_s = turn_ref[0], turn_ref[1]
    for p in range(2):
        halves = [x_ref[k:k + 128] + x_ref[k + 128:k + 256] for k in (512 * p, 512 * p + 256)]
        values = jnp.concatenate(halves, 0)
        both = mul(first_ref[...], jnp.concatenate(split(values), 1), NN)
        part = both[:512, :128] + (both[:512, 128:] + both[512:, :128])
        part_c, part_s = part[:256], part[256:]
        turned = jnp.concatenate(
            [part_c * turn_c - part_s * turn_s, part_c * turn_s + part_s * turn_c], 1
        )
        high, low = split(turned)
        both = mul(last_ref[...], high, NT)
        field = both[:128] + both[128:] + mul(last_ref[:128, :], low, NT)
        for side in range(2):
            values = jnp.exp(-(field[:, 128 * side:128 * side + 128] + mean_ref[p, 0:1, :]))
            total = total + values[:64] + values[64:]
    coarse = -jnp.log(total * 0.125)
    group = lax.broadcasted_iota(jnp.int32, (16, 128), 1) // 32
    blocks = [coarse[16 * ly:16 * ly + 16] for ly in range(4)]
    for q in range(4):
        row = blocks[q]
        for ly in range(4):
            if ly != q:
                row = jnp.where(group == ly, pltpu.roll(blocks[ly], (ly - q) * 32 % 128, 1), row)
        o_ref[:, q, :] = row[:8]
        o_ref[:, 7 - q, :] = row[8:]


def place_kernel(x_ref, table_ref, o_ref):
    values = x_ref[...].T
    high = values.astype(BF16)
    middle, low = split(values - high.astype(F32))
    out = jnp.zeros((32, 256), F32)
    for ly in range(4):
        rows = slice(32 * ly, 32 * ly + 32)
        parts = jnp.concatenate([high[rows], middle[rows], low[rows]], 0)
        spread = mul(parts, table_ref[:, 256 * ly:256 * ly + 256], NN)
        out = out + (spread[:32] + (spread[32:64] + spread[64:]))
    back = lax.axis_index("gx") // 4 % 2
    for r in range(32):
        o_ref[pl.ds(jnp.where(back == 1, 31 - r, r), 1), :] = out[r:r + 1]


def call(kernel, shapes, places, scratch=()):
    spaces = {"s": pltpu.SMEM, "v": pltpu.VMEM}
    outs = [jax.ShapeDtypeStruct(shape, F32) for shape in shapes]
    result = pl.pallas_call(
        kernel,
        out_shape=outs,
        in_specs=[pl.BlockSpec(memory_space=spaces[place]) for place in places],
        out_specs=[pl.BlockSpec(memory_space=pltpu.VMEM)] * len(outs),
        scratch_shapes=list(scratch),
        compiler_params=pltpu.CompilerParams(vmem_limit_bytes=32 * 1024 * 1024),
    )
    return lambda *operands: result(*operands)


def body(normals, plane_length, plane_amplitude, plane_mean):
    sides = [[2 * y + h for y in range(4)] for h in range(2)]
    lines = lax.all_to_all(
        normals.reshape(4, 32, 512), "gy", 0, 0, tiled=True, axis_index_groups=sides
    )
    scratch = [pltpu.VMEM((512, 128), F32), pltpu.VMEM((4, 32, 8, 256), F32)]
    rows, mean = call(y_kernel, [(1024, 128), (2, 8, 128)], "sssvv", scratch)(
        plane_length, plane_amplitude, plane_mean, lines, y_tables()
    )
    rows = lax.all_to_all(rows.reshape(512, 2, 128), ("gy", "gx"), 0, 0, tiled=True)
    first, turn, last = x_tables()
    (coarse,) = call(x_kernel, [(8, 8, 128)], "vvvvv")(
        mean, rows.reshape(1024, 128), first, turn, last
    )
    coarse = lax.all_to_all(coarse.reshape(64, 1, 128), "gx", 0, 0, tiled=True)
    (out,) = call(place_kernel, [(32, 256)], "vv")(coarse.reshape(64, 128), place_table())
    return out.reshape(1, 1, 32, 256)


def solution(mesh):
    return jax.shard_map(
        body,
        mesh=mesh,
        in_specs=(P(None, None, "gx", "gy"), P(), P(), P()),
        out_specs=P(None, None, "gx", "gy"),
        check_vma=False,
    )
```

```python
import math

import jax
import jax.numpy as jnp
import numpy as np
from jax import lax
from jax.experimental import pallas as pl
from jax.experimental.pallas import tpu as pltpu
from jax.sharding import PartitionSpec as P

F32 = jnp.float32
BF16 = jnp.bfloat16
NX = 4096
NY = 4096
GX = 64
GY = 8
NN = (((1,), (0,)), ((), ()))
NT = (((1,), (1,)), ((), ()))


def np_split(table):
    high = table.astype(np.float32).astype(jnp.bfloat16)
    low = (table - high.astype(np.float64)).astype(np.float32).astype(jnp.bfloat16)
    return high, low


def split(values):
    high = values.astype(BF16)
    low = (values - high.astype(F32)).astype(BF16)
    return high, low


def mul(left, right, dims):
    return lax.dot_general(left, right, dims, preferred_element_type=F32)


def angles(top, period):
    return np.pi * (top % (2 * period)).astype(np.float64) / period


def y_tables():
    outer, inner = 32, 128
    a = np.arange(outer).reshape(4, 2, 4).transpose(1, 0, 2).reshape(1, outer)
    l = np.arange(outer)[:, None]
    phase = angles(a * (2 * l + 1), 2 * outer)
    high, low = [t.astype(np.float64) for t in np_split(np.concatenate([np.cos(phase), np.sin(phase)], 0))]
    b = np.arange(inner)[None, :]
    turn = angles(b * (2 * l + 1), 2 * NY)
    turn = np.concatenate([np.cos(turn), np.sin(turn)], 1)
    j, sub = np.meshgrid(np.arange(GY), np.arange(16), indexing="ij")
    m = np.where(sub < 8, 8 * j + sub, 127 - 8 * j - (sub - 8)).reshape(-1, 1)
    last = angles(2 * b * m, inner)
    last = np.concatenate([np.cos(last), -np.sin(last)], 1)
    packed = np.zeros((288, 256))
    for h in range(2):
        own = slice(16 * h, 16 * h + 16)
        packed[64 * h:64 * h + 64, :48] = np.concatenate([high[:, own], high[:, own], low[:, own]], 1)
    packed[128:160] = turn
    packed[160:] = last
    return packed.astype(np.float32)


def x_tables():
    outer, inner = 256, 16
    l = np.concatenate([np.arange(0, outer, 2), np.arange(1, outer, 2)])[:, None]
    a = np.arange(outer).reshape(64, 2, 2).transpose(1, 0, 2).reshape(1, outer)
    phase = angles(a * (2 * l + 1), 2 * outer)
    first = np.concatenate(np_split(np.concatenate([np.cos(phase), np.sin(phase)], 0)), 0)
    lanes = np.arange(128)[None, :]
    b = lanes // 8
    turn = angles(b * (2 * l + 1), 2 * NX)
    turn = np.stack([np.cos(turn), np.sin(turn)]).astype(np.float32)
    index = np.arange(128)[:, None]
    fine = index // 16 % 4 * 2 + index // 64
    m = np.concatenate([np.arange(8), np.arange(15, 7, -1)])[index % 16]
    same = 1.0 * (lanes % 8 == fine)
    phase = angles(2 * b * m, inner)
    last = np.concatenate([same * np.cos(phase), -same * np.sin(phase)], 1)
    return first, turn, np.concatenate(np_split(last), 0)


def place_table():
    src = np.arange(GX)
    octet, sub = src // 16, src % 16
    table = np.zeros((GX, 4, 256), np.float32)
    for ly in range(4):
        column = np.where(sub < 8, 32 * sub + 4 * octet + ly, 32 * (sub - 8) + 31 - 4 * octet - ly)
        table[src, ly, column] = 1
    return table.reshape(GX, 1024).astype(jnp.bfloat16)


def y_kernel(length, amplitude, mean, x_ref, table_ref, o_ref, mean_ref, s_ref, w_ref):
    gx, gy = lax.axis_index("gx"), lax.axis_index("gy")
    plane, half = gy // 4, gy % 2
    norming = math.sqrt(2.0 * math.pi) / math.sqrt(NX * NY)
    reach = math.pi * length[plane]
    factor = amplitude[plane] * length[plane] * norming * math.sqrt(2.0 / NY)
    row = gx * 64 + gy // 2 % 2 * 32 + lax.broadcasted_iota(jnp.int32, (32, 128), 0)
    row_part = reach * (row.astype(F32) * (1.0 / NX))
    row_part = 1.0 + row_part * row_part
    scale = factor * jnp.where(row == 0, math.sqrt(1.0 / NX), math.sqrt(2.0 / NX))
    lane = lax.broadcasted_iota(jnp.int32, (8, 128), 1)
    for a in range(16):
        col = (a // 4 * 8 + half * 4 + a % 4) * 128 + lane
        col_part = reach * (col.astype(F32) * (1.0 / NY))
        col_part = col_part * col_part
        root = lax.rsqrt(row_part + jnp.concatenate([col_part] * 4, 0))
        spectrum = root * root * lax.rsqrt(root) * scale
        if a == 0:
            first_col = jnp.where(col == 0, math.sqrt(0.5), 1.0).astype(F32)
            spectrum = spectrum * jnp.concatenate([first_col] * 4, 0)
        s_ref[32 * a:32 * a + 32, :] = x_ref[a // 4, :, a % 4 * 128:a % 4 * 128 + 128] * spectrum
    for p in range(2):
        mean_ref[p] = jnp.full((8, 128), mean[p], F32)
    first = table_ref[pl.ds(pl.multiple_of(half * 64, 64), 64), :128].astype(BF16)[:, :48]
    turn_c, turn_s = table_ref[128:160, :128], table_ref[128:160, 128:]
    last = jnp.concatenate(split(table_ref[160:288, :]), 0)
    for group in range(4):
        pieces = []
        for line in range(8 * group, 8 * group + 8):
            high, low = split(s_ref[pl.ds(line, 16, stride=32), :])
            pieces.append(jnp.concatenate([high, low, high], 0))
        part = mul(first, jnp.concatenate(pieces, 1), NN)
        for k in range(8):
            part_c, part_s = part[:32, k * 128:(k + 1) * 128], part[32:, k * 128:(k + 1) * 128]
            line = 8 * group + k
            w_ref[:, line, :, :128] = (part_c * turn_c - part_s * turn_s).reshape(4, 8, 128)
            w_ref[:, line, :, 128:] = (part_c * turn_s + part_s * turn_c).reshape(4, 8, 128)
    for octet in range(4):
        high, low = split(w_ref[octet].reshape(256, 256))
        both = mul(last, high, NT)
        out = both[:128] + both[128:] + mul(last[:128], low, NT)
        for j in range(GY):
            for side in range(2):
                block = out[16 * j:16 * j + 16, 128 * side:128 * side + 128]
                o_ref[pl.ds(128 * j + 32 * octet + side, 16, stride=2), :] = block


def x_kernel(mean_ref, x_ref, first_ref, turn_ref, last_ref, o_ref):
    total = jnp.zeros((64, 128), F32)
    turn_c, turn_s = turn_ref[0], turn_ref[1]
    planes = []
    for p in range(2):
        halves = [x_ref[k:k + 128] + x_ref[k + 128:k + 256] for k in (512 * p, 512 * p + 256)]
        planes.append(jnp.concatenate(halves, 0))
    high, low = split(jnp.concatenate(planes, 1))
    both = mul(first_ref[...], high, NN)
    part = both[:512] + (both[512:] + mul(first_ref[:512, :], low, NN))
    for p in range(2):
        part_c, part_s = part[:256, 128 * p:128 * p + 128], part[256:, 128 * p:128 * p + 128]
        turned = jnp.concatenate(
            [part_c * turn_c - part_s * turn_s, part_c * turn_s + part_s * turn_c], 1
        )
        high, low = split(turned)
        both = mul(last_ref[...], high, NT)
        field = both[:128] + both[128:] + mul(last_ref[:128, :], low, NT)
        for side in range(2):
            values = jnp.exp(-(field[:, 128 * side:128 * side + 128] + mean_ref[p, 0:1, :]))
            total = total + values[:64] + values[64:]
    coarse = -jnp.log(total * 0.125)
    group = lax.broadcasted_iota(jnp.int32, (16, 128), 1) // 32
    blocks = [coarse[16 * ly:16 * ly + 16] for ly in range(4)]
    for q in range(4):
        row = blocks[q]
        for ly in range(4):
            if ly != q:
                row = jnp.where(group == ly, pltpu.roll(blocks[ly], (ly - q) * 32 % 128, 1), row)
        o_ref[:, q, :] = row[:8]
        o_ref[:, 7 - q, :] = row[8:]


def place_kernel(x_ref, table_ref, o_ref):
    values = x_ref[...].T
    high = values.astype(BF16)
    middle, low = split(values - high.astype(F32))
    out = jnp.zeros((32, 256), F32)
    for ly in range(4):
        rows = slice(32 * ly, 32 * ly + 32)
        parts = jnp.concatenate([high[rows], middle[rows], low[rows]], 0)
        spread = mul(parts, table_ref[:, 256 * ly:256 * ly + 256], NN)
        out = out + (spread[:32] + (spread[32:64] + spread[64:]))
    back = lax.axis_index("gx") // 4 % 2
    for r in range(32):
        o_ref[pl.ds(jnp.where(back == 1, 31 - r, r), 1), :] = out[r:r + 1]


def call(kernel, shapes, places, scratch=()):
    spaces = {"s": pltpu.SMEM, "v": pltpu.VMEM}
    outs = [jax.ShapeDtypeStruct(shape, F32) for shape in shapes]
    result = pl.pallas_call(
        kernel,
        out_shape=outs,
        in_specs=[pl.BlockSpec(memory_space=spaces[place]) for place in places],
        out_specs=[pl.BlockSpec(memory_space=pltpu.VMEM)] * len(outs),
        scratch_shapes=list(scratch),
        compiler_params=pltpu.CompilerParams(vmem_limit_bytes=32 * 1024 * 1024),
    )
    return lambda *operands: result(*operands)


def body(normals, plane_length, plane_amplitude, plane_mean):
    sides = [[2 * y + h for y in range(4)] for h in range(2)]
    lines = lax.all_to_all(
        normals.reshape(4, 32, 512), "gy", 0, 0, tiled=True, axis_index_groups=sides
    )
    scratch = [pltpu.VMEM((512, 128), F32), pltpu.VMEM((4, 32, 8, 256), F32)]
    rows, mean = call(y_kernel, [(1024, 128), (2, 8, 128)], "sssvv", scratch)(
        plane_length, plane_amplitude, plane_mean, lines, y_tables()
    )
    rows = lax.all_to_all(rows.reshape(512, 2, 128), ("gy", "gx"), 0, 0, tiled=True)
    first, turn, last = x_tables()
    (coarse,) = call(x_kernel, [(8, 8, 128)], "vvvvv")(
        mean, rows.reshape(1024, 128), first, turn, last
    )
    coarse = lax.all_to_all(coarse.reshape(64, 1, 128), "gx", 0, 0, tiled=True)
    (out,) = call(place_kernel, [(32, 256)], "vv")(coarse.reshape(64, 128), place_table())
    return out.reshape(1, 1, 32, 256)


def solution(mesh):
    return jax.shard_map(
        body,
        mesh=mesh,
        in_specs=(P(None, None, "gx", "gy"), P(), P(), P()),
        out_specs=P(None, None, "gx", "gy"),
        check_vma=False,
    )
```

```python
import math

import jax
import jax.numpy as jnp
import numpy as np
from jax import lax
from jax.experimental import pallas as pl
from jax.experimental.pallas import tpu as pltpu
from jax.sharding import PartitionSpec as P

F32 = jnp.float32
BF16 = jnp.bfloat16
NX = 4096
NY = 4096
GX = 64
GY = 8
NN = (((1,), (0,)), ((), ()))
NT = (((1,), (1,)), ((), ()))


def np_split(table):
    high = table.astype(np.float32).astype(jnp.bfloat16)
    low = (table - high.astype(np.float64)).astype(np.float32).astype(jnp.bfloat16)
    return high, low


def split(values):
    high = values.astype(BF16)
    low = (values - high.astype(F32)).astype(BF16)
    return high, low


def mul(left, right, dims):
    return lax.dot_general(left, right, dims, preferred_element_type=F32)


def angles(top, period):
    return np.pi * (top % (2 * period)).astype(np.float64) / period


def y_tables():
    outer, inner = 32, 128
    a = np.arange(outer).reshape(4, 2, 4).transpose(1, 0, 2).reshape(1, outer)
    l = np.arange(outer)[:, None]
    phase = angles(a * (2 * l + 1), 2 * outer)
    high, low = [t.astype(np.float64) for t in np_split(np.concatenate([np.cos(phase), np.sin(phase)], 0))]
    b = np.arange(inner)[None, :]
    turn = angles(b * (2 * l + 1), 2 * NY)
    turn = np.concatenate([np.cos(turn), np.sin(turn)], 1)
    j, sub = np.meshgrid(np.arange(GY), np.arange(16), indexing="ij")
    m = np.where(sub < 8, 8 * j + sub, 127 - 8 * j - (sub - 8)).reshape(-1, 1)
    last = angles(2 * b * m, inner)
    last = np.concatenate([np.cos(last), -np.sin(last)], 1)
    packed = np.zeros((288, 256))
    for h in range(2):
        own = slice(16 * h, 16 * h + 16)
        packed[64 * h:64 * h + 64, :48] = np.concatenate([high[:, own], high[:, own], low[:, own]], 1)
    packed[128:160] = turn
    packed[160:] = last
    return packed.astype(np.float32)


def x_tables():
    outer, inner = 256, 16
    l = np.concatenate([np.arange(0, outer, 2), np.arange(1, outer, 2)])[:, None]
    a = np.arange(outer).reshape(64, 2, 2).transpose(1, 0, 2).reshape(1, outer)
    phase = angles(a * (2 * l + 1), 2 * outer)
    first = np.concatenate(np_split(np.concatenate([np.cos(phase), np.sin(phase)], 0)), 0)
    lanes = np.arange(128)[None, :]
    b = lanes // 8
    turn = angles(b * (2 * l + 1), 2 * NX)
    turn = np.stack([np.cos(turn), np.sin(turn)]).astype(np.float32)
    index = np.arange(128)[:, None]
    fine = index // 16 % 4 * 2 + index // 64
    m = np.concatenate([np.arange(8), np.arange(15, 7, -1)])[index % 16]
    same = 1.0 * (lanes % 8 == fine)
    phase = angles(2 * b * m, inner)
    last = np.concatenate([same * np.cos(phase), -same * np.sin(phase)], 1)
    return first, turn, np.concatenate(np_split(last), 0)


def place_table():
    src = np.arange(GX)
    octet, sub = src // 16, src % 16
    table = np.zeros((GX, 4, 256), np.float32)
    for ly in range(4):
        column = np.where(sub < 8, 32 * sub + 4 * octet + ly, 32 * (sub - 8) + 31 - 4 * octet - ly)
        table[src, ly, column] = 1
    return table.reshape(GX, 1024).astype(jnp.bfloat16)


def y_kernel(length, amplitude, mean, x_ref, table_ref, o_ref, mean_ref, s_ref, w_ref):
    gx, gy = lax.axis_index("gx"), lax.axis_index("gy")
    plane, half = gy // 4, gy % 2
    norming = math.sqrt(2.0 * math.pi) / math.sqrt(NX * NY)
    own_length, own_amplitude = [
        jnp.where(plane == 0, values[:, 0:1], values[:, 1:2])
        for values in (length[...].reshape(1, 2), amplitude[...].reshape(1, 2))
    ]
    reach = math.pi * own_length
    factor = own_amplitude * own_length * (norming * math.sqrt(2.0 / NY))
    row = gx * 64 + gy // 2 % 2 * 32 + lax.broadcasted_iota(jnp.int32, (32, 128), 0)
    row_part = reach * (row.astype(F32) * (1.0 / NX))
    row_part = 1.0 + row_part * row_part
    scale = factor * jnp.where(row == 0, math.sqrt(1.0 / NX), math.sqrt(2.0 / NX))
    lane = lax.broadcasted_iota(jnp.int32, (8, 128), 1)
    for a in range(16):
        col = (a // 4 * 8 + half * 4 + a % 4) * 128 + lane
        col_part = reach * (col.astype(F32) * (1.0 / NY))
        col_part = col_part * col_part
        root = lax.rsqrt(row_part + jnp.concatenate([col_part] * 4, 0))
        spectrum = root * root * lax.rsqrt(root) * scale
        if a == 0:
            first_col = jnp.where(col == 0, math.sqrt(0.5), 1.0).astype(F32)
            spectrum = spectrum * jnp.concatenate([first_col] * 4, 0)
        s_ref[32 * a:32 * a + 32, :] = x_ref[a // 4, :, a % 4 * 128:a % 4 * 128 + 128] * spectrum
    values = mean[...].reshape(1, 2)
    for p in range(2):
        mean_ref[p] = jnp.broadcast_to(values[:, p:p + 1], (8, 128))
    first = table_ref[pl.ds(pl.multiple_of(half * 64, 64), 64), :128].astype(BF16)[:, :48]
    turn_c, turn_s = table_ref[128:160, :128], table_ref[128:160, 128:]
    last = jnp.concatenate(split(table_ref[160:288, :]), 0)
    for group in range(4):
        pieces = []
        for line in range(8 * group, 8 * group + 8):
            high, low = split(s_ref[pl.ds(line, 16, stride=32), :])
            pieces.append(jnp.concatenate([high, low, high], 0))
        part = mul(first, jnp.concatenate(pieces, 1), NN)
        for k in range(8):
            part_c, part_s = part[:32, k * 128:(k + 1) * 128], part[32:, k * 128:(k + 1) * 128]
            line = 8 * group + k
            w_ref[:, line, :, :128] = (part_c * turn_c - part_s * turn_s).reshape(4, 8, 128)
            w_ref[:, line, :, 128:] = (part_c * turn_s + part_s * turn_c).reshape(4, 8, 128)
    for octet in range(4):
        high, low = split(w_ref[octet].reshape(256, 256))
        both = mul(last, high, NT)
        out = both[:128] + both[128:] + mul(last[:128], low, NT)
        for j in range(GY):
            for side in range(2):
                block = out[16 * j:16 * j + 16, 128 * side:128 * side + 128]
                o_ref[pl.ds(128 * j + 32 * octet + side, 16, stride=2), :] = block


def x_kernel(mean_ref, x_ref, first_ref, turn_ref, last_ref, o_ref):
    total = jnp.zeros((64, 128), F32)
    turn_c, turn_s = turn_ref[0], turn_ref[1]
    planes = []
    for p in range(2):
        halves = [x_ref[k:k + 128] + x_ref[k + 128:k + 256] for k in (512 * p, 512 * p + 256)]
        planes.append(jnp.concatenate(halves, 0))
    high, low = split(jnp.concatenate(planes, 1))
    both = mul(first_ref[...], high, NN)
    part = both[:512] + (both[512:] + mul(first_ref[:512, :], low, NN))
    for p in range(2):
        part_c, part_s = part[:256, 128 * p:128 * p + 128], part[256:, 128 * p:128 * p + 128]
        turned = jnp.concatenate(
            [part_c * turn_c - part_s * turn_s, part_c * turn_s + part_s * turn_c], 1
        )
        high, low = split(turned)
        both = mul(last_ref[...], high, NT)
        field = both[:128] + both[128:] + mul(last_ref[:128, :], low, NT)
        for side in range(2):
            values = jnp.exp(-(field[:, 128 * side:128 * side + 128] + mean_ref[p, 0:1, :]))
            total = total + values[:64] + values[64:]
    coarse = -jnp.log(total * 0.125)
    group = lax.broadcasted_iota(jnp.int32, (16, 128), 1) // 32
    blocks = [coarse[16 * ly:16 * ly + 16] for ly in range(4)]
    for q in range(4):
        row = blocks[q]
        for ly in range(4):
            if ly != q:
                row = jnp.where(group == ly, pltpu.roll(blocks[ly], (ly - q) * 32 % 128, 1), row)
        o_ref[:, q, :] = row[:8]
        o_ref[:, 7 - q, :] = row[8:]


def place_kernel(x_ref, table_ref, o_ref):
    values = x_ref[...].T
    high = values.astype(BF16)
    middle, low = split(values - high.astype(F32))
    out = jnp.zeros((32, 256), F32)
    for ly in range(4):
        rows = slice(32 * ly, 32 * ly + 32)
        parts = jnp.concatenate([high[rows], middle[rows], low[rows]], 0)
        spread = mul(parts, table_ref[:, 256 * ly:256 * ly + 256], NN)
        out = out + (spread[:32] + (spread[32:64] + spread[64:]))
    back = lax.axis_index("gx") // 4 % 2
    for r in range(32):
        o_ref[pl.ds(jnp.where(back == 1, 31 - r, r), 1), :] = out[r:r + 1]


def call(kernel, shapes, inputs, scratch=()):
    outs = [jax.ShapeDtypeStruct(shape, F32) for shape in shapes]
    result = pl.pallas_call(
        kernel,
        out_shape=outs,
        in_specs=[pl.BlockSpec(memory_space=pltpu.VMEM)] * inputs,
        out_specs=[pl.BlockSpec(memory_space=pltpu.VMEM)] * len(outs),
        scratch_shapes=list(scratch),
        compiler_params=pltpu.CompilerParams(vmem_limit_bytes=32 * 1024 * 1024),
    )
    return lambda *operands: result(*operands)


def body(normals, plane_length, plane_amplitude, plane_mean):
    sides = [[2 * y + h for y in range(4)] for h in range(2)]
    lines = lax.all_to_all(
        normals.reshape(4, 32, 512), "gy", 0, 0, tiled=True, axis_index_groups=sides
    )
    scratch = [pltpu.VMEM((512, 128), F32), pltpu.VMEM((4, 32, 8, 256), F32)]
    rows, mean = call(y_kernel, [(1024, 128), (2, 8, 128)], 5, scratch)(
        plane_length, plane_amplitude, plane_mean, lines, y_tables()
    )
    rows = lax.all_to_all(rows.reshape(512, 2, 128), ("gy", "gx"), 0, 0, tiled=True)
    first, turn, last = x_tables()
    (coarse,) = call(x_kernel, [(8, 8, 128)], 5)(
        mean, rows.reshape(1024, 128), first, turn, last
    )
    coarse = lax.all_to_all(coarse.reshape(64, 1, 128), "gx", 0, 0, tiled=True)
    (out,) = call(place_kernel, [(32, 256)], 2)(coarse.reshape(64, 128), place_table())
    return out.reshape(1, 1, 32, 256)


def solution(mesh):
    return jax.shard_map(
        body,
        mesh=mesh,
        in_specs=(P(None, None, "gx", "gy"), P(), P(), P()),
        out_specs=P(None, None, "gx", "gy"),
        check_vma=False,
    )
```

```python
import math

import jax
import jax.numpy as jnp
import numpy as np
from jax import lax
from jax.experimental import pallas as pl
from jax.experimental.pallas import tpu as pltpu
from jax.sharding import PartitionSpec as P

F32 = jnp.float32
BF16 = jnp.bfloat16
NX = 4096
NY = 4096
GX = 64
GY = 8
NN = (((1,), (0,)), ((), ()))
NT = (((1,), (1,)), ((), ()))


def np_split(table):
    high = table.astype(np.float32).astype(jnp.bfloat16)
    low = (table - high.astype(np.float64)).astype(np.float32).astype(jnp.bfloat16)
    return high, low


def split(values):
    high = values.astype(BF16)
    low = (values - high.astype(F32)).astype(BF16)
    return high, low


def mul(left, right, dims):
    return lax.dot_general(left, right, dims, preferred_element_type=F32)


def angles(top, period):
    return np.pi * (top % (2 * period)).astype(np.float64) / period


def y_tables():
    outer, inner = 32, 128
    a = np.arange(outer).reshape(4, 2, 4).transpose(1, 0, 2).reshape(1, outer)
    l = np.arange(outer)[:, None]
    phase = angles(a * (2 * l + 1), 2 * outer)
    high, low = [t.astype(np.float64) for t in np_split(np.concatenate([np.cos(phase), np.sin(phase)], 0))]
    b = np.arange(inner)[None, :]
    turn = angles(b * (2 * l + 1), 2 * NY)
    turn = np.concatenate([np.cos(turn), np.sin(turn)], 1)
    j, sub = np.meshgrid(np.arange(GY), np.arange(16), indexing="ij")
    m = np.where(sub < 8, 8 * j + sub, 127 - 8 * j - (sub - 8)).reshape(-1, 1)
    last = angles(2 * b * m, inner)
    last = np.concatenate([np.cos(last), -np.sin(last)], 1)
    packed = np.zeros((288, 256))
    for h in range(2):
        own = slice(16 * h, 16 * h + 16)
        packed[64 * h:64 * h + 64, :48] = np.concatenate([high[:, own], high[:, own], low[:, own]], 1)
    packed[128:160] = turn
    packed[160:] = last
    return packed.astype(np.float32)


def x_tables():
    outer, inner = 256, 16
    l = np.concatenate([np.arange(0, outer, 2), np.arange(1, outer, 2)])[:, None]
    a = np.arange(outer).reshape(64, 2, 2).transpose(1, 0, 2).reshape(1, outer)
    phase = angles(a * (2 * l + 1), 2 * outer)
    first = np.concatenate(np_split(np.concatenate([np.cos(phase), np.sin(phase)], 0)), 0)
    lanes = np.arange(128)[None, :]
    b = lanes // 8
    turn = angles(b * (2 * l + 1), 2 * NX)
    turn = np.stack([np.cos(turn), np.sin(turn)]).astype(np.float32)
    index = np.arange(128)[:, None]
    fine = index // 16 % 4 * 2 + index // 64
    m = np.concatenate([np.arange(8), np.arange(15, 7, -1)])[index % 16]
    same = 1.0 * (lanes % 8 == fine)
    phase = angles(2 * b * m, inner)
    last = np.concatenate([same * np.cos(phase), -same * np.sin(phase)], 1)
    return first, turn, np.concatenate(np_split(last), 0)


def place_table():
    src = np.arange(GX)
    octet, sub = src // 16, src % 16
    table = np.zeros((GX, 4, 256), np.float32)
    for ly in range(4):
        column = np.where(sub < 8, 32 * sub + 4 * octet + ly, 32 * (sub - 8) + 31 - 4 * octet - ly)
        table[src, ly, column] = 1
    return table.reshape(GX, 1024).astype(jnp.bfloat16)


def y_kernel(length, amplitude, mean, x_ref, table_ref, o_ref, mean_ref, s_ref, w_ref, sent_ref):
    gx, gy = lax.axis_index("gx"), lax.axis_index("gy")
    plane, half = gy // 4, gy % 2
    norming = math.sqrt(2.0 * math.pi) / math.sqrt(NX * NY)
    own_length, own_amplitude = [
        jnp.where(plane == 0, values[:, 0:1], values[:, 1:2])
        for values in (length[...].reshape(1, 2), amplitude[...].reshape(1, 2))
    ]
    reach = math.pi * own_length
    factor = own_amplitude * own_length * (norming * math.sqrt(2.0 / NY))
    row = gx * 64 + gy // 2 % 2 * 32 + lax.broadcasted_iota(jnp.int32, (32, 128), 0)
    row_part = reach * (row.astype(F32) * (1.0 / NX))
    row_part = 1.0 + row_part * row_part
    scale = factor * jnp.where(row == 0, math.sqrt(1.0 / NX), math.sqrt(2.0 / NX))
    lane = lax.broadcasted_iota(jnp.int32, (8, 128), 1)
    for a in range(16):
        col = (a // 4 * 8 + half * 4 + a % 4) * 128 + lane
        col_part = reach * (col.astype(F32) * (1.0 / NY))
        col_part = col_part * col_part
        root = lax.rsqrt(row_part + jnp.concatenate([col_part] * 4, 0))
        spectrum = root * root * lax.rsqrt(root) * scale
        if a == 0:
            first_col = jnp.where(col == 0, math.sqrt(0.5), 1.0).astype(F32)
            spectrum = spectrum * jnp.concatenate([first_col] * 4, 0)
        s_ref[32 * a:32 * a + 32, :] = x_ref[a // 4, :, a % 4 * 128:a % 4 * 128 + 128] * spectrum
    values = mean[...].reshape(1, 2)
    for p in range(2):
        mean_ref[p] = jnp.broadcast_to(values[:, p:p + 1], (8, 128))
    first = table_ref[pl.ds(pl.multiple_of(half * 64, 64), 64), :128].astype(BF16)[:, :48]
    turn_c, turn_s = table_ref[128:160, :128], table_ref[128:160, 128:]
    last = jnp.concatenate(split(table_ref[160:288, :]), 0)
    for group in range(4):
        pieces = []
        for line in range(8 * group, 8 * group + 8):
            high, low = split(s_ref[pl.ds(line, 16, stride=32), :])
            pieces.append(jnp.concatenate([high, low, high], 0))
        part = mul(first, jnp.concatenate(pieces, 1), NN)
        for k in range(8):
            part_c, part_s = part[:32, k * 128:(k + 1) * 128], part[32:, k * 128:(k + 1) * 128]
            line = 8 * group + k
            w_ref[:, line, :, :128] = (part_c * turn_c - part_s * turn_s).reshape(4, 8, 128)
            w_ref[:, line, :, 128:] = (part_c * turn_s + part_s * turn_c).reshape(4, 8, 128)
    for octet in range(4):
        high, low = split(w_ref[octet].reshape(256, 256))
        both = mul(last, high, NT)
        out = both[:128] + both[128:] + mul(last[:128], low, NT)
        for j in range(GY):
            for side in range(2):
                block = out[16 * j:16 * j + 16, 128 * side:128 * side + 128]
                sent_ref[pl.ds(128 * j + 32 * octet + side, 16, stride=2), :] = block
    o_ref[...] = sent_ref[:1024, :]


def x_kernel(mean_ref, x_ref, first_ref, turn_ref, last_ref, o_ref):
    total = jnp.zeros((64, 128), F32)
    turn_c, turn_s = turn_ref[0], turn_ref[1]
    planes = []
    for p in range(2):
        halves = [x_ref[k:k + 128] + x_ref[k + 128:k + 256] for k in (512 * p, 512 * p + 256)]
        planes.append(jnp.concatenate(halves, 0))
    high, low = split(jnp.concatenate(planes, 1))
    both = mul(first_ref[...], high, NN)
    part = both[:512] + (both[512:] + mul(first_ref[:512, :], low, NN))
    for p in range(2):
        part_c, part_s = part[:256, 128 * p:128 * p + 128], part[256:, 128 * p:128 * p + 128]
        turned = jnp.concatenate(
            [part_c * turn_c - part_s * turn_s, part_c * turn_s + part_s * turn_c], 1
        )
        high, low = split(turned)
        both = mul(last_ref[...], high, NT)
        field = both[:128] + both[128:] + mul(last_ref[:128, :], low, NT)
        for side in range(2):
            values = jnp.exp(-(field[:, 128 * side:128 * side + 128] + mean_ref[p, 0:1, :]))
            total = total + values[:64] + values[64:]
    coarse = -jnp.log(total * 0.125)
    group = lax.broadcasted_iota(jnp.int32, (16, 128), 1) // 32
    blocks = [coarse[16 * ly:16 * ly + 16] for ly in range(4)]
    for q in range(4):
        row = blocks[q]
        for ly in range(4):
            if ly != q:
                row = jnp.where(group == ly, pltpu.roll(blocks[ly], (ly - q) * 32 % 128, 1), row)
        o_ref[:, q, :] = row[:8]
        o_ref[:, 7 - q, :] = row[8:]


def place_kernel(x_ref, table_ref, o_ref):
    values = x_ref[...].T
    high = values.astype(BF16)
    middle, low = split(values - high.astype(F32))
    out = jnp.zeros((32, 256), F32)
    for ly in range(4):
        rows = slice(32 * ly, 32 * ly + 32)
        parts = jnp.concatenate([high[rows], middle[rows], low[rows]], 0)
        spread = mul(parts, table_ref[:, 256 * ly:256 * ly + 256], NN)
        out = out + (spread[:32] + (spread[32:64] + spread[64:]))
    back = lax.axis_index("gx") // 4 % 2
    for r in range(32):
        o_ref[pl.ds(jnp.where(back == 1, 31 - r, r), 1), :] = out[r:r + 1]


def call(kernel, shapes, inputs, scratch=()):
    outs = [jax.ShapeDtypeStruct(shape, F32) for shape in shapes]
    result = pl.pallas_call(
        kernel,
        out_shape=outs,
        in_specs=[pl.BlockSpec(memory_space=pltpu.VMEM)] * inputs,
        out_specs=[pl.BlockSpec(memory_space=pltpu.VMEM)] * len(outs),
        scratch_shapes=list(scratch),
        compiler_params=pltpu.CompilerParams(vmem_limit_bytes=32 * 1024 * 1024),
    )
    return lambda *operands: result(*operands)


def body(normals, plane_length, plane_amplitude, plane_mean):
    sides = [[2 * y + h for y in range(4)] for h in range(2)]
    lines = lax.all_to_all(
        normals.reshape(4, 32, 512), "gy", 0, 0, tiled=True, axis_index_groups=sides
    )
    scratch = [
        pltpu.VMEM(shape, F32) for shape in ((544, 128), (4, 32, 8, 256), (1032, 128))
    ]
    rows, mean = call(y_kernel, [(1024, 128), (2, 8, 128)], 5, scratch)(
        plane_length, plane_amplitude, plane_mean, lines, y_tables()
    )
    rows = lax.all_to_all(rows.reshape(512, 2, 128), ("gy", "gx"), 0, 0, tiled=True)
    first, turn, last = x_tables()
    (coarse,) = call(x_kernel, [(8, 8, 128)], 5)(
        mean, rows.reshape(1024, 128), first, turn, last
    )
    coarse = lax.all_to_all(coarse.reshape(64, 1, 128), "gx", 0, 0, tiled=True)
    (out,) = call(place_kernel, [(32, 256)], 2)(coarse.reshape(64, 128), place_table())
    return out.reshape(1, 1, 32, 256)


def solution(mesh):
    return jax.shard_map(
        body,
        mesh=mesh,
        in_specs=(P(None, None, "gx", "gy"), P(), P(), P()),
        out_specs=P(None, None, "gx", "gy"),
        check_vma=False,
    )
```
